512 devices in a mesh: gx: 32 (over z_lo, x), gy: 8 (over y, z_hi), gz: 2 (over core).
Axes of the slice: x: 4, y: 4, z: 16 (z_hi: 2, z_lo: 8; z = z_hi * 8 + z_lo), core: 2. Of those that a mesh axis runs over, the one named last changes fastest.
Arguments:
- velocity_term: float32 [128, 256, 256], P('gx', 'gy', 'gz'), may hold values from 0.05 to 0.2
- model_step: float32 [128, 256, 256], P('gx', 'gy', 'gz'), may hold values from -6 to 6
- background: bfloat16 [4, 128, 256, 256], P(None, 'gx', 'gy', 'gz'), may hold values from -6 to 6
- receivers: int32 [3, 256], replicated, may hold values from 0 to 255, as said below
- checkpoints: int32 [16], replicated, may hold values from 0 to 3, as said below
Outputs:
- image: float32 [128, 256, 256], P('gx', 'gy', 'gz')
- traces: float32 [16, 256], replicated
- column_image: float32 [128, 256], P('gx', 'gy')
- wavefield: float32 [128, 256, 256], P('gx', 'gy', 'gz')
The draws below stay inside these ranges and needn't reach their ends.
Inputs may be any that keep to these rules, and one draw needn't show every extreme that they name: receivers[0] indexes the first lateral dimension (below 128), receivers[1] the second (below 256), receivers[2] depth (below 256). `checkpoints`: never falling over the time steps, beginning at 0 and ending at 3.
All inputs are finite; a program needn't handle non-finite values.
Results may differ from the reference program's by a relative error of at most 0.0003.
Values sent between devices are 32-bit elements; how exact they have to be, the bound alone decides.
No kernel may reach another device: no remote copies, remote signals or barrier semaphores. Data moves between devices by JAX's collectives and lax.ppermute only.
A program may use at most 64 MiB of HBM per device.

```python
import jax
import jax.numpy as jnp
from jax import lax

NT = 16
NCK = 4
RECV = 256
NX = 128
NY = 256
NZ = 256


def draw_receivers(key, part):
    key_x = jax.random.fold_in(key, 11)
    key_y = jax.random.fold_in(key, 12)
    key_z = jax.random.fold_in(key, 13)
    first = jax.random.randint(key_x, (RECV,), 0, NX)
    second = jax.random.randint(key_y, (RECV,), 0, NY)
    third = jax.random.randint(key_z, (RECV,), 0, NZ)
    return jnp.stack([first, second, third]).astype(jnp.int32)


def draw_checkpoints(key, part):
    inner = jax.random.fold_in(key, 21)
    values = jnp.sort(jax.random.randint(inner, (NT,), 0, NCK))
    values = values.at[0].set(0).at[NT - 1].set(NCK - 1)
    return values.astype(jnp.int32)


def block_levels(key, shape, pieces, smallest, top_value):
    gain, own = 1.0, jax.random.fold_in(key, 6)
    for dim, shards_of in pieces:
        steps = jnp.exp(jax.random.uniform(jax.random.fold_in(own, dim), (shards_of,), jnp.float32, smallest / len(pieces), top_value / len(pieces)))
        gain = gain * jnp.repeat(steps, shape[dim] // shards_of).reshape([-1 if axis == dim else 1 for axis in range(len(shape))])
    return gain


def centred(rng, dims, width, most, cuts=(), kind=jnp.bfloat16):
    array = width * jax.random.normal(rng, dims, jnp.float32)
    if cuts:
        array = array * block_levels(rng, dims, cuts, -0.22, 0.18)
    return jnp.clip(array, -most, most).astype(kind)


def setup_inputs(seed: int = 0) -> dict:
    seeds = jax.random.split(jax.random.key(seed), 6)
    return {
        "velocity_term": jnp.clip(0.05 + 0.15 * jax.random.uniform(seeds[0], (NX, NY, NZ), jnp.float32) ** block_levels(seeds[0], (NX, NY, NZ), ((0, 32), (1, 8), (2, 2)), -0.2, 0.2), 0.05, 0.2),
        "model_step": centred(seeds[1], (NX, NY, NZ), 1.0, 6.0, ((0, 32), (1, 8), (2, 2)), jnp.float32),
        "background": centred(seeds[2], (NCK, NX, NY, NZ), 1.0, 6.0, ((1, 32), (2, 8), (3, 2))),
        "receivers": draw_receivers(jax.random.fold_in(seeds[5], 71), 0),
        "checkpoints": draw_checkpoints(jax.random.fold_in(seeds[5], 71), 0),
    }


near_coef = 4.0 / 3.0
far_coef = -1.0 / 12.0
center_coef = -2.5


def laplace(field):
    total = 3.0 * center_coef * field
    for dim in (0, 1):
        total = total + near_coef * (jnp.roll(field, 1, dim) + jnp.roll(field, -1, dim))
        total = total + far_coef * (jnp.roll(field, 2, dim) + jnp.roll(field, -2, dim))
    padded = jnp.pad(field, ((0, 0), (0, 0), (2, 2)))
    total = total + near_coef * (padded[:, :, 3:-1] + padded[:, :, 1:-3])
    total = total + far_coef * (padded[:, :, 4:] + padded[:, :, :-4])
    return total


def reference(velocity_term, model_step, background, receivers, checkpoints):
    rec_x = receivers[0]
    rec_y = receivers[1]
    rec_z = receivers[2]
    zeros = jnp.zeros(model_step.shape, jnp.float32)
    previous = zeros
    current = zeros
    samples = []
    for step in range(NT):
        accel = lax.dynamic_index_in_dim(background, checkpoints[step], 0, keepdims=False).astype(jnp.float32)
        following = 2.0 * current - previous + velocity_term * laplace(current) + model_step * accel
        samples.append(following[rec_x, rec_y, rec_z])
        previous = current
        current = following
    traces = jnp.stack(samples)
    wavefield = current
    later_two = zeros
    later = zeros
    image = zeros
    for back in range(NT):
        step = NT - 1 - back
        accel = lax.dynamic_index_in_dim(background, checkpoints[step], 0, keepdims=False).astype(jnp.float32)
        adjoint = 2.0 * later - later_two + laplace(velocity_term * later)
        adjoint = adjoint.at[rec_x, rec_y, rec_z].add(traces[step])
        image = image + adjoint * accel
        later_two = later
        later = adjoint
    column_image = jnp.sum(image, axis=2) / NZ
    return image, traces, column_image, wavefield
```

```python
import functools

import jax
import jax.numpy as jnp
from jax import lax
from jax.experimental import pallas as pl
from jax.experimental.pallas import tpu as pltpu
from jax.sharding import Mesh
from jax.sharding import PartitionSpec as P

AXES = ("zl", "x", "y", "zh", "c")
SIZES = (8, 4, 4, 2, 2)
B = 8
R = 3 * B
PAD = 8
NT = 16
near_coef = 4.0 / 3.0
far_coef = -1.0 / 12.0
center_coef = -7.5


def linear(x, y, z, c):
    return ((((z % 8) * 4 + x) * 4 + y) * 2 + z // 8) * 2 + c


def table(place):
    out = []
    for x in range(4):
        for y in range(4):
            for z in range(16):
                for c in range(2):
                    out.append((linear(x, y, z, c), linear(*place(x, y, z, c))))
    return sorted(out)


def shifted(dx=0, dy=0, dz=0, dc=0):
    return table(lambda x, y, z, c: ((x + dx) % 4, (y + dy) % 4, (z + dz) % 16, (c + dc) % 2))


def spread(other):
    def place(x, y, z, c):
        zl, zh = z % 8, z // 8
        return (2 * zh + ((x & 1) ^ other), y, 2 * zl + (x >> 1), c)

    return table(place)


def across(x, y, z, c):
    index = (4 * y + x + (1 if c else -1)) % 16
    return (index % 4, index // 4, z, 1 - c)


SWAP = shifted(dc=1)
ACROSS = table(across)
UP = shifted(dz=1)
DOWN = shifted(dz=-1)


def send(value, pairs):
    return lax.ppermute(value, AXES, pairs)


def back(pairs):
    return sorted((target, source) for source, target in pairs)


def lane_ids():
    return lax.broadcasted_iota(jnp.int32, (8, 128), 1)


def laplace_tile(buf, x, row):
    lane = lane_ids()
    here, near, far = [], [], []
    for half in range(2):
        here.append(buf[x, half, row : row + 8, :])
        near.append(
            (buf[x - 1, half, row : row + 8, :] + buf[x + 1, half, row : row + 8, :])
            + (buf[x, half, row - 1 : row + 7, :] + buf[x, half, row + 1 : row + 9, :])
        )
        far.append(
            (buf[x - 2, half, row : row + 8, :] + buf[x + 2, half, row : row + 8, :])
            + (buf[x, half, row - 2 : row + 6, :] + buf[x, half, row + 2 : row + 10, :])
        )
    low, high = here
    up1 = [pltpu.roll(v, 127, 1) for v in here]
    up2 = [pltpu.roll(v, 126, 1) for v in here]
    dn1 = [pltpu.roll(v, 1, 1) for v in here]
    dn2 = [pltpu.roll(v, 2, 1) for v in here]
    near[0] += jnp.where(lane < 127, up1[0], up1[1]) + jnp.where(lane >= 1, dn1[0], 0.0)
    near[1] += jnp.where(lane < 127, up1[1], 0.0) + jnp.where(lane >= 1, dn1[1], dn1[0])
    far[0] += jnp.where(lane < 126, up2[0], up2[1]) + jnp.where(lane >= 2, dn2[0], 0.0)
    far[1] += jnp.where(lane < 126, up2[1], 0.0) + jnp.where(lane >= 2, dn2[1], dn2[0])
    return here, [
        near_coef * near[h] + far_coef * far[h] + center_coef * here[h] for h in range(2)
    ]


def tiles_for(margin):
    return (PAD, PAD + 8, PAD + 16) if margin > 0 else (PAD + 8,)


def assemble(buf, f, mid, inter, intra, core):
    buf[:, :, PAD + 8 : PAD + 16, :] = mid[f]

    @pl.when(core == 0)
    def _():
        buf[:, :, PAD : PAD + 8, :] = inter[f]
        buf[:, :, PAD + 16 : PAD + 24, :] = intra[f]

    @pl.when(core == 1)
    def _():
        buf[:, :, PAD : PAD + 8, :] = intra[f]
        buf[:, :, PAD + 16 : PAD + 24, :] = inter[f]


def own(buf):
    return buf[B : 2 * B, :, PAD + 8 : PAD + 16, :]


def sample(buf, step, place, receivers, mine, counts, traces):
    lane = lax.broadcasted_iota(jnp.int32, (1, 128), 1)
    lanes = lax.broadcasted_iota(jnp.int32, (1, 256), 1)

    def body(i, _):
        r = mine[i]
        x = receivers[0, r] - place[0] + B
        y = receivers[1, r] - place[1] + PAD + 8
        z = receivers[2, r]
        row = buf[x, z // 128, pl.ds(y, 1), :]
        value = jnp.sum(jnp.where(lane == z % 128, row, 0.0))
        traces[step : step + 1, :] = jnp.where(lanes == r, value, traces[step : step + 1, :])
        return 0

    lax.fori_loop(0, counts[0], body, 0)


def forward_steps(steps, a, b, vel, src, place, checkpoints, receivers, mine, counts, traces):
    for done, step in enumerate(steps):
        margin = 2 * (len(steps) - 1 - done)
        ck = checkpoints[step]

        def plane(x, _, a=a, b=b, margin=margin, ck=ck):
            for row in tiles_for(margin):
                here, lap = laplace_tile(b, x, row)
                for half in range(2):
                    at = (x, half, slice(row, row + 8), slice(None))
                    cell = (x, half, slice(row - PAD, row - PAD + 8), slice(None))
                    a[at] = (
                        2.0 * here[half] - a[at] + vel[cell] * lap[half] + src[(ck, *cell)]
                    )
            return 0

        lax.fori_loop(B - margin, 2 * B + margin, plane, 0)
        a, b = b, a
        sample(b, step, place, receivers, mine, counts, traces)
    return a, b


def first_forward(
    place, checkpoints, receivers, mine, counts, mid, inter, intra, vel, src, pair, traces, a, b
):
    core = place[2]
    for f in range(5):
        into = vel if f == 0 else src.at[f - 1]
        into[:, :, 8:16, :] = mid[f]

        @pl.when(core == 0)
        def _():
            into[:, :, 0:8, :] = inter[f]
            into[:, :, 16:24, :] = intra[f]

        @pl.when(core == 1)
        def _():
            into[:, :, 0:8, :] = intra[f]
            into[:, :, 16:24, :] = inter[f]

    traces[...] = jnp.zeros_like(traces)
    a[...] = jnp.zeros_like(a)
    b[:, :, PAD : PAD + R, :] = src[checkpoints[0]]
    sample(b, 0, place, receivers, mine, counts, traces)
    prev, cur = forward_steps(
        range(1, 5), a, b, vel, src, place, checkpoints, receivers, mine, counts, traces
    )
    pair[0] = own(prev)
    pair[1] = own(cur)


def later_forward(
    steps, place, checkpoints, receivers, mine, counts, vel, src, mid, inter, intra, held,
    pair, traces, a, b,
):
    assemble(a, 0, mid, inter, intra, place[2])
    assemble(b, 1, mid, inter, intra, place[2])
    traces[...] = held[...]
    prev, cur = forward_steps(
        steps, a, b, vel, src, place, checkpoints, receivers, mine, counts, traces
    )
    pair[0] = own(prev)
    pair[1] = own(cur)


def inject(buf, step, place, receivers, near, counts, traces):
    lane = lax.broadcasted_iota(jnp.int32, (1, 128), 1)

    def body(i, _):
        r = near[i]
        x = (receivers[0, r] - place[0] + B) & 127
        y = ((receivers[1, r] - place[1] + B) & 255) + PAD
        z = receivers[2, r]
        half = z // 128
        row = buf[x, half, pl.ds(y, 1), :]
        buf[x, half, pl.ds(y, 1), :] = row + jnp.where(lane == z % 128, traces[step, r], 0.0)
        return 0

    lax.fori_loop(0, counts[1], body, 0)


def add_image(image, buf, back_own, ck):
    image[...] += own(buf) * back_own[ck]


def adjoint_steps(
    steps, a, b, w, vel, back_own, place, checkpoints, receivers, near, counts, traces, image
):
    for done, step in enumerate(steps):
        margin = 2 * (len(steps) - 1 - done)

        def scale(x, _, b=b):
            for row in tiles_for(1):
                for half in range(2):
                    at = (x, half, slice(row, row + 8), slice(None))
                    w[at] = b[at] * vel[x, half, row - PAD : row - PAD + 8, :]
            return 0

        lax.fori_loop(B - margin - 2, 2 * B + margin + 2, scale, 0)

        def plane(x, _, a=a, b=b, margin=margin):
            for row in tiles_for(margin):
                _, lap = laplace_tile(w, x, row)
                for half in range(2):
                    at = (x, half, slice(row, row + 8), slice(None))
                    a[at] = 2.0 * b[at] - a[at] + lap[half]
            return 0

        lax.fori_loop(B - margin, 2 * B + margin, plane, 0)
        a, b = b, a
        inject(b, step, place, receivers, near, counts, traces)
        add_image(image, b, back_own, checkpoints[step])
    return a, b


def first_adjoint(
    place, checkpoints, receivers, near, counts, traces, vel, back_own, pair, image, a, b, w
):
    a[...] = jnp.zeros_like(a)
    b[...] = jnp.zeros_like(b)
    image[...] = jnp.zeros_like(image)
    inject(b, NT - 1, place, receivers, near, counts, traces)
    add_image(image, b, back_own, checkpoints[NT - 1])
    later, now = adjoint_steps(
        range(14, 10, -1), a, b, w, vel, back_own, place, checkpoints, receivers, near, counts,
        traces, image,
    )
    pair[0] = own(later)
    pair[1] = own(now)


def later_adjoint(
    steps, place, checkpoints, receivers, near, counts, traces, vel, back_own, mid, inter, intra,
    held, pair, image, a, b, w,
):
    assemble(a, 0, mid, inter, intra, place[2])
    assemble(b, 1, mid, inter, intra, place[2])
    image[...] = held[...]
    later, now = adjoint_steps(
        steps, a, b, w, vel, back_own, place, checkpoints, receivers, near, counts, traces, image
    )
    pair[0] = own(later)
    pair[1] = own(now)


def list_receivers(place, receivers, mine, near, counts):
    counts[0] = 0
    counts[1] = 0

    def body(r, _):
        x = (receivers[0, r] - place[0] + B) & 127
        y = (receivers[1, r] - place[1] + B) & 255

        @pl.when((x < R) & (y < R))
        def _():
            n = counts[1]
            near[n] = r
            counts[1] = n + 1

            @pl.when((x >= B) & (x < 2 * B) & (y >= B) & (y < 2 * B))
            def _():
                m = counts[0]
                mine[m] = r
                counts[0] = m + 1

        return 0

    lax.fori_loop(0, 256, body, 0)


SM = pl.BlockSpec(memory_space=pltpu.SMEM)
VM = pl.BlockSpec(memory_space=pltpu.VMEM)
FIELD = (R, 2, R + 2 * PAD, 128)


def f32(*shape):
    return jax.ShapeDtypeStruct(shape, jnp.float32)


def i32(*shape):
    return jax.ShapeDtypeStruct(shape, jnp.int32)


def call(body, ins, outs, out_specs, fields):
    return pl.pallas_call(
        body,
        in_specs=ins,
        out_specs=out_specs,
        out_shape=outs,
        scratch_shapes=[pltpu.VMEM(FIELD, jnp.float32)] * fields,
        compiler_params=pltpu.CompilerParams(vmem_limit_bytes=48 * 1024 * 1024),
    )


def exchange(block):
    low = send(block, UP)
    high = send(block, DOWN)
    mid = jnp.concatenate([low, block, high], axis=1)
    return mid, send(mid, ACROSS), send(mid, SWAP)


def pick(two, index):
    return jnp.where(index == 0, two[0], two[1])


def ordered(first, second, index, axis):
    return jnp.where(
        index == 0, jnp.stack([first, second], axis), jnp.stack([second, first], axis)
    )


def inward(stacked, core, odd):
    count = stacked.shape[0]
    rows = stacked.reshape(count, 4, 2, 2, 8, 128)
    even, uneven = rows[:, :, :, 0], rows[:, :, :, 1]
    kept = pick((even, uneven), core)
    came = send(pick((uneven, even), core), SWAP)
    whole = ordered(kept, came, core, 3)
    first, second = whole[:, :, 0], whole[:, :, 1]
    got = send(pick((first, second), odd), spread(0))
    other = send(pick((second, first), odd), spread(1))
    return ordered(got, other, odd, 1).reshape(count, 8, 2, 8, 128)


def outward(block, core, odd):
    first, second = block[:4], block[4:]
    got = send(pick((first, second), odd), back(spread(0)))
    other = send(pick((second, first), odd), back(spread(1)))
    whole = ordered(got, other, odd, 1)
    front, rear = whole[:, :, 0], whole[:, :, 1]
    kept = pick((front, rear), core)
    came = send(pick((rear, front), core), SWAP)
    return ordered(kept, came, core, 2).reshape(4, 32, 128)


def merge(*parts):
    total = parts[0]
    for part in parts[1:]:
        total = jnp.where(total == 0.0, part, total)
    return total


def on_device(velocity_term, model_step, background, receivers, checkpoints):
    core = lax.axis_index("c")
    x = lax.axis_index("x")
    y = lax.axis_index("y")
    z = lax.axis_index("zh") * 8 + lax.axis_index("zl")
    odd = x & 1
    place = jnp.stack([B * z, 16 * (4 * y + x) + B * core, core, core]).astype(jnp.int32)
    mine, near, counts = pl.pallas_call(
        list_receivers,
        in_specs=[SM, SM],
        out_specs=[SM, SM, SM],
        out_shape=[i32(256), i32(256), i32(2)],
    )(place, receivers)
    stacked = jnp.concatenate(
        [velocity_term[None], model_step[None], background.astype(jnp.float32)], axis=0
    )
    inner = inward(stacked, core, odd)
    back_own = inner[2:]
    fields = jnp.concatenate([inner[:1], inner[1:2] * back_own], axis=0)
    vel, src, pair, traces = call(
        first_forward,
        [SM] * 5 + [VM] * 3,
        [f32(R, 2, R, 128), f32(4, R, 2, R, 128), f32(2, B, 2, B, 128), f32(NT, 256)],
        [VM] * 4,
        2,
    )(place, checkpoints, receivers, mine, counts, *exchange(fields))
    for steps in (range(5, 9), range(9, 13), range(13, 16)):
        pair, traces = call(
            functools.partial(later_forward, steps),
            [SM] * 5 + [VM] * 6,
            [f32(2, B, 2, B, 128), f32(NT, 256)],
            [VM] * 2,
            2,
        )(place, checkpoints, receivers, mine, counts, vel, src, *exchange(pair), traces)
    wavefield = outward(pair[1], core, odd)
    traces = merge(traces, send(traces, UP), send(traces, DOWN))
    traces = merge(traces, send(traces, ACROSS), send(traces, SWAP))
    local = traces
    traces = merge(traces, send(traces, shifted(dz=3)), send(traces, shifted(dz=-3)))
    traces = merge(traces, send(traces, shifted(dz=8)))
    traces = merge(traces, send(traces, shifted(dx=1)))
    traces = merge(traces, send(traces, shifted(dx=2)))
    traces = merge(traces, send(traces, shifted(dy=1)))
    traces = merge(traces, send(traces, shifted(dy=2)))
    scalars = (place, checkpoints, receivers, near, counts, local)
    pair, image = call(
        first_adjoint,
        [SM] * 6 + [VM] * 2,
        [f32(2, B, 2, B, 128), f32(B, 2, B, 128)],
        [VM] * 2,
        3,
    )(*scalars, vel, back_own)
    for steps in (range(10, 6, -1), range(6, 2, -1), range(2, -1, -1)):
        pair, image = call(
            functools.partial(later_adjoint, steps),
            [SM] * 6 + [VM] * 6,
            [f32(2, B, 2, B, 128), f32(B, 2, B, 128)],
            [VM] * 2,
            3,
        )(*scalars, vel, back_own, *exchange(pair), image)
    image = outward(image, core, odd)
    column_image = lax.psum(jnp.sum(image, axis=2), "c") / 256.0
    return (image, traces, column_image, wavefield)


def solution(mesh):
    torus = Mesh(mesh.devices.reshape(SIZES), AXES)
    across_x, across_y = ("zl", "x"), ("y", "zh")
    return jax.shard_map(
        on_device,
        mesh=torus,
        in_specs=(
            P(across_x, across_y, "c"),
            P(across_x, across_y, "c"),
            P(None, across_x, across_y, "c"),
            P(),
            P(),
        ),
        out_specs=(
            P(across_x, across_y, "c"),
            P(),
            P(across_x, across_y),
            P(across_x, across_y, "c"),
        ),
        check_vma=False,
    )
```

```python
import functools

import jax
import jax.numpy as jnp
from jax import lax
from jax.experimental import pallas as pl
from jax.experimental.pallas import tpu as pltpu
from jax.sharding import Mesh
from jax.sharding import PartitionSpec as P

AXES = ("zl", "x", "y", "zh", "c")
SIZES = (8, 4, 4, 2, 2)
B = 8
R = 3 * B
PAD = 8
NT = 16


def linear(x, y, z, c):
    return ((((z % 8) * 4 + x) * 4 + y) * 2 + z // 8) * 2 + c


def table(place):
    out = []
    for x in range(4):
        for y in range(4):
            for z in range(16):
                for c in range(2):
                    out.append((linear(x, y, z, c), linear(*place(x, y, z, c))))
    return sorted(out)


def shifted(dx=0, dy=0, dz=0, dc=0):
    return table(lambda x, y, z, c: ((x + dx) % 4, (y + dy) % 4, (z + dz) % 16, (c + dc) % 2))


def spread(other):
    def place(x, y, z, c):
        zl, zh = z % 8, z // 8
        return (2 * zh + ((x & 1) ^ other), y, 2 * zl + (x >> 1), c)

    return table(place)


def across(x, y, z, c):
    index = (4 * y + x + (1 if c else -1)) % 16
    return (index % 4, index // 4, z, 1 - c)


SWAP = shifted(dc=1)
ACROSS = table(across)
UP = shifted(dz=1)
DOWN = shifted(dz=-1)


def send(value, pairs):
    return lax.ppermute(value, AXES, pairs)


def back(pairs):
    return sorted((target, source) for source, target in pairs)


def merge(*parts):
    total = parts[0]
    for part in parts[1:]:
        total = jnp.where(total == 0.0, part, total)
    return total


def band():
    row = lax.broadcasted_iota(jnp.int32, (256, 256), 0)
    gap = jnp.abs(row - lax.broadcasted_iota(jnp.int32, (256, 256), 1))
    one = jnp.where(gap == 1, 16.0, jnp.where(gap == 2, -1.0, 0.0)).astype(jnp.bfloat16)
    return jnp.concatenate([one, one], axis=0)


def depth_part(buf, deep, bands, margin):
    first, count = B - margin, B + 2 * margin
    low, size = (PAD, R) if margin > 0 else (PAD + 8, 8)
    field = jnp.concatenate(
        [
            buf[first : first + count, half, low : low + size, :].reshape(count * size, 128)
            for half in range(2)
        ],
        axis=1,
    )
    high = field.astype(jnp.bfloat16)
    rest = (field - high.astype(jnp.float32)).astype(jnp.bfloat16)
    out = jnp.dot(
        jnp.concatenate([high, rest], axis=1), bands[...], preferred_element_type=jnp.float32
    )
    for half in range(2):
        deep[first : first + count, half, low - PAD : low - PAD + size, :] = out[
            :, 128 * half : 128 * half + 128
        ].reshape(count, size, 128)


def laplace_tile(buf, deep, x, half, row):
    here = buf[x, half, row : row + 8, :]
    near = (buf[x - 1, half, row : row + 8, :] + buf[x + 1, half, row : row + 8, :]) + (
        buf[x, half, row - 1 : row + 7, :] + buf[x, half, row + 1 : row + 9, :]
    )
    far = (buf[x - 2, half, row : row + 8, :] + buf[x + 2, half, row : row + 8, :]) + (
        buf[x, half, row - 2 : row + 6, :] + buf[x, half, row + 2 : row + 10, :]
    )
    depth = deep[x, half, row - PAD : row - PAD + 8, :]
    return here, (16.0 * near - far) + (depth - 90.0 * here)


def tiles_for(margin):
    return (PAD, PAD + 8, PAD + 16) if margin > 0 else (PAD + 8,)


def assemble(buf, f, mid, intra, inter, core):
    buf[:, :, PAD + 8 : PAD + 16, :] = mid[f, :R]

    @pl.when(core == 0)
    def _():
        buf[:, :, PAD : PAD + 8, :] = inter[f, :R]
        buf[:, :, PAD + 16 : PAD + 24, :] = intra[f, :R]

    @pl.when(core == 1)
    def _():
        buf[:, :, PAD : PAD + 8, :] = intra[f, :R]
        buf[:, :, PAD + 16 : PAD + 24, :] = inter[f, :R]


def own(buf):
    return buf[B : 2 * B, :, PAD + 8 : PAD + 16, :]


def sample(buf, step, place, receivers, mine, counts, traces):
    lane = lax.broadcasted_iota(jnp.int32, (1, 128), 1)
    lanes = lax.broadcasted_iota(jnp.int32, (1, 256), 1)

    def body(i, _):
        r = mine[i]
        x = receivers[0, r] - place[0] + B
        y = receivers[1, r] - place[1] + PAD + 8
        z = receivers[2, r]
        row = buf[x, z // 128, pl.ds(y, 1), :]
        value = jnp.sum(jnp.where(lane == z % 128, row, 0.0))
        traces[step : step + 1, :] = jnp.where(lanes == r, value, traces[step : step + 1, :])
        return 0

    lax.fori_loop(0, counts[0], body, 0)


def forward_steps(steps, a, b, deep, bands, vel, src, place, checkpoints, receivers, mine, counts, traces):
    for done, step in enumerate(steps):
        margin = 2 * (len(steps) - 1 - done)
        ck = checkpoints[step]

        depth_part(b, deep, bands, margin)

        def plane(x, _, a=a, b=b, margin=margin, ck=ck):
            for row in tiles_for(margin):
                for half in range(2):
                    here, lap = laplace_tile(b, deep, x, half, row)
                    at = (x, half, slice(row, row + 8), slice(None))
                    cell = (x, half, slice(row - PAD, row - PAD + 8), slice(None))
                    a[at] = 2.0 * here - a[at] + vel[cell] * lap + src[(ck, *cell)]
            return 0

        lax.fori_loop(B - margin, 2 * B + margin, plane, 0)
        a, b = b, a
        sample(b, step, place, receivers, mine, counts, traces)
    return a, b


def first_forward(
    place, checkpoints, receivers, mine, counts, mid, intra, inter, vel, src, pair, traces, a, b, deep, bands
):
    core = place[2]
    for f in range(5):
        into = vel if f == 0 else src.at[f - 1]
        into[:, :, 8:16, :] = mid[f]

        @pl.when(core == 0)
        def _():
            into[:, :, 0:8, :] = inter[f]
            into[:, :, 16:24, :] = intra[f]

        @pl.when(core == 1)
        def _():
            into[:, :, 0:8, :] = intra[f]
            into[:, :, 16:24, :] = inter[f]

    bands[...] = band()
    traces[...] = jnp.zeros_like(traces)
    a[...] = jnp.zeros_like(a)
    b[:, :, PAD : PAD + R, :] = src[checkpoints[0]]
    sample(b, 0, place, receivers, mine, counts, traces)
    prev, cur = forward_steps(
        range(1, 5), a, b, deep, bands, vel, src, place, checkpoints, receivers, mine, counts, traces
    )
    pair[0] = own(prev)
    pair[1] = own(cur)


def later_forward(
    steps, place, checkpoints, receivers, mine, counts, vel, src, mid, intra, inter, held,
    pair, traces, a, b, deep, bands,
):
    assemble(a, 0, mid, intra, inter, place[2])
    assemble(b, 1, mid, intra, inter, place[2])
    bands[...] = band()
    traces[...] = held[...]
    prev, cur = forward_steps(
        steps, a, b, deep, bands, vel, src, place, checkpoints, receivers, mine, counts, traces
    )
    pair[0] = own(prev)
    pair[1] = own(cur)


def inject(buf, step, place, receivers, near, counts, traces):
    lane = lax.broadcasted_iota(jnp.int32, (1, 128), 1)

    def body(i, _):
        r = near[i]
        x = (receivers[0, r] - place[0] + B) & 127
        y = ((receivers[1, r] - place[1] + B) & 255) + PAD
        z = receivers[2, r]
        half = z // 128
        row = buf[x, half, pl.ds(y, 1), :]
        buf[x, half, pl.ds(y, 1), :] = row + jnp.where(lane == z % 128, traces[step, r], 0.0)
        return 0

    lax.fori_loop(0, counts[1], body, 0)


def add_image(image, buf, back_own, ck):
    image[...] += own(buf) * back_own[ck]


def adjoint_steps(
    steps, a, b, w, deep, bands, vel, back_own, place, checkpoints, receivers, near, counts, traces, image
):
    for done, step in enumerate(steps):
        margin = 2 * (len(steps) - 1 - done)

        def scale(x, _, b=b):
            for row in tiles_for(1):
                for half in range(2):
                    at = (x, half, slice(row, row + 8), slice(None))
                    w[at] = b[at] * vel[x, half, row - PAD : row - PAD + 8, :]
            return 0

        lax.fori_loop(B - margin - 2, 2 * B + margin + 2, scale, 0)

        depth_part(w, deep, bands, margin)

        def plane(x, _, a=a, b=b, margin=margin):
            for row in tiles_for(margin):
                for half in range(2):
                    _, lap = laplace_tile(w, deep, x, half, row)
                    at = (x, half, slice(row, row + 8), slice(None))
                    a[at] = 2.0 * b[at] - a[at] + lap
            return 0

        lax.fori_loop(B - margin, 2 * B + margin, plane, 0)
        a, b = b, a
        inject(b, step, place, receivers, near, counts, traces)
        add_image(image, b, back_own, checkpoints[step])
    return a, b


def first_adjoint(
    place, checkpoints, receivers, near, counts, traces, vel, back_own, carried, pair, image, a, b, w, deep, bands
):
    a[...] = jnp.zeros_like(a)
    b[...] = jnp.zeros_like(b)
    image[...] = jnp.zeros_like(image)
    bands[...] = band()
    inject(b, NT - 1, place, receivers, near, counts, traces)
    add_image(image, b, back_own, checkpoints[NT - 1])
    later, now = adjoint_steps(
        range(14, 10, -1), a, b, w, deep, bands, vel, back_own, place, checkpoints, receivers, near, counts,
        traces, image,
    )
    for f, buf in enumerate((later, now)):
        pair[f, :B] = own(buf)
        pair[f, B] = carried[f]


def later_adjoint(
    steps, place, checkpoints, receivers, near, counts, traces, vel, back_own, mid, intra, inter,
    held, far, pair, image, a, b, w, deep, bands,
):
    assemble(a, 0, mid, intra, inter, place[2])
    assemble(b, 1, mid, intra, inter, place[2])
    image[...] = held[...]
    bands[...] = band()
    later, now = adjoint_steps(
        steps, a, b, w, deep, bands, vel, back_own, place, checkpoints, receivers, near, counts, traces, image
    )
    for f, buf in enumerate((later, now)):
        pair[f, :B] = own(buf)
        pair[f, B] = merge(mid[f, R], intra[f, R], inter[f, R], far[f])


def list_receivers(place, receivers, mine, near, counts):
    counts[0] = 0
    counts[1] = 0

    def body(r, _):
        x = (receivers[0, r] - place[0] + B) & 127
        y = (receivers[1, r] - place[1] + B) & 255

        @pl.when((x < R) & (y < R))
        def _():
            n = counts[1]
            near[n] = r
            counts[1] = n + 1

            @pl.when((x >= B) & (x < 2 * B) & (y >= B) & (y < 2 * B))
            def _():
                m = counts[0]
                mine[m] = r
                counts[0] = m + 1

        return 0

    lax.fori_loop(0, 256, body, 0)


SM = pl.BlockSpec(memory_space=pltpu.SMEM)
VM = pl.BlockSpec(memory_space=pltpu.VMEM)
FIELD = (R, 2, R + 2 * PAD, 128)


def f32(*shape):
    return jax.ShapeDtypeStruct(shape, jnp.float32)


def i32(*shape):
    return jax.ShapeDtypeStruct(shape, jnp.int32)


def call(body, ins, outs, out_specs, fields):
    return pl.pallas_call(
        body,
        in_specs=ins,
        out_specs=out_specs,
        out_shape=outs,
        scratch_shapes=[pltpu.VMEM(FIELD, jnp.float32)] * fields
        + [pltpu.VMEM((R, 2, R, 128), jnp.float32), pltpu.VMEM((512, 256), jnp.bfloat16)],
        compiler_params=pltpu.CompilerParams(vmem_limit_bytes=48 * 1024 * 1024),
    )


def exchange(block):
    low = send(block, UP)
    high = send(block, DOWN)
    mid = jnp.concatenate([low, block, high], axis=1)
    return mid, send(mid, SWAP), send(mid, ACROSS)


def exchange_carrying(block, more, beside):
    low = send(block, UP)
    high = send(block, DOWN)
    known = merge(block[:, B:], low[:, B:], high[:, B:], more[:, None])
    mid = jnp.concatenate([low[:, :B], block[:, :B], high[:, :B], known], axis=1)
    mid, beside = lax.optimization_barrier((mid, beside))
    return (mid, send(mid, SWAP), send(mid, ACROSS)), beside


def pick(two, index):
    return jnp.where(index == 0, two[0], two[1])


def ordered(first, second, index, axis):
    return jnp.where(
        index == 0, jnp.stack([first, second], axis), jnp.stack([second, first], axis)
    )


def inward(stacked, core, odd):
    count = stacked.shape[0]
    rows = stacked.reshape(count, 4, 2, 2, 8, 128)
    even, uneven = rows[:, :, :, 0], rows[:, :, :, 1]
    kept = pick((even, uneven), core)
    came = send(pick((uneven, even), core), SWAP)
    whole = ordered(kept, came, core, 3)
    first, second = whole[:, :, 0], whole[:, :, 1]
    got = send(pick((first, second), odd), spread(0))
    other = send(pick((second, first), odd), spread(1))
    return ordered(got, other, odd, 1).reshape(count, 8, 2, 8, 128)


def outward_far(block, odd):
    first, second = block[:4], block[4:]
    got = send(pick((first, second), odd), back(spread(0)))
    return got, send(pick((second, first), odd), back(spread(1)))


def outward_near(got, other, core, odd):
    whole = ordered(got, other, odd, 1)
    front, rear = whole[:, :, 0], whole[:, :, 1]
    kept = pick((front, rear), core)
    came = send(pick((rear, front), core), SWAP)
    return ordered(kept, came, core, 2).reshape(4, 32, 128)


def on_device(velocity_term, model_step, background, receivers, checkpoints):
    core = lax.axis_index("c")
    x = lax.axis_index("x")
    y = lax.axis_index("y")
    z = lax.axis_index("zh") * 8 + lax.axis_index("zl")
    odd = x & 1
    place = jnp.stack([B * z, 16 * (4 * y + x) + B * core, core, core]).astype(jnp.int32)
    mine, near, counts = pl.pallas_call(
        list_receivers,
        in_specs=[SM, SM],
        out_specs=[SM, SM, SM],
        out_shape=[i32(256), i32(256), i32(2)],
    )(place, receivers)
    stacked = jnp.concatenate(
        [velocity_term[None] * (1.0 / 12.0), model_step[None], background.astype(jnp.float32)], axis=0
    )
    inner = inward(stacked, core, odd)
    back_own = inner[2:]
    fields = jnp.concatenate([inner[:1], inner[1:2] * back_own], axis=0)
    vel, src, pair, traces = call(
        first_forward,
        [SM] * 5 + [VM] * 3,
        [f32(R, 2, R, 128), f32(4, R, 2, R, 128), f32(2, B, 2, B, 128), f32(NT, 256)],
        [VM] * 4,
        2,
    )(place, checkpoints, receivers, mine, counts, *exchange(fields))
    for steps in (range(5, 9), range(9, 13), range(13, 16)):
        pair, traces = call(
            functools.partial(later_forward, steps),
            [SM] * 5 + [VM] * 6,
            [f32(2, B, 2, B, 128), f32(NT, 256)],
            [VM] * 2,
            2,
        )(place, checkpoints, receivers, mine, counts, vel, src, *exchange(pair), traces)
    field = pair[1]
    local = merge(traces, send(traces, UP), send(traces, DOWN))
    local = merge(local, send(local, ACROSS), send(local, SWAP))
    carried = local.reshape(2, 8, 2, 128).transpose(0, 2, 1, 3)
    swapped = send(carried, SWAP)
    scalars = (place, checkpoints, receivers, near, counts, local)
    outs = [f32(2, B + 1, 2, B, 128), f32(B, 2, B, 128)]
    pair, image = call(first_adjoint, [SM] * 6 + [VM] * 3, outs, [VM] * 2, 3)(
        *scalars, vel, back_own, carried
    )
    beside = ()
    for number, steps in enumerate((range(10, 6, -1), range(6, 2, -1), range(2, -1, -1))):
        parts, beside = exchange_carrying(pair, swapped, beside)
        if number == 0:
            far = send(parts[0][:, R], shifted(dz=8))
            beside = (field,)
        elif number == 1:
            far = carried
            beside = outward_far(beside[0], odd)
        else:
            wavefield = outward_near(*beside, core, odd)
        pair, image = call(
            functools.partial(later_adjoint, steps), [SM] * 6 + [VM] * 7, outs, [VM] * 2, 3
        )(*scalars, vel, back_own, *parts, image, far)
    carried = pair[:, B]
    carried = merge(carried, send(carried, shifted(dy=1)))
    carried = merge(carried, send(carried, shifted(dy=2)))
    traces = carried.transpose(0, 2, 1, 3).reshape(NT, 256)
    image = outward_near(*outward_far(image, odd), core, odd)
    column_image = lax.psum(jnp.sum(image, axis=2), "c") / 256.0
    return (image, traces, column_image, wavefield)


def solution(mesh):
    torus = Mesh(mesh.devices.reshape(SIZES), AXES)
    across_x, across_y = ("zl", "x"), ("y", "zh")
    return jax.shard_map(
        on_device,
        mesh=torus,
        in_specs=(
            P(across_x, across_y, "c"),
            P(across_x, across_y, "c"),
            P(None, across_x, across_y, "c"),
            P(),
            P(),
        ),
        out_specs=(
            P(across_x, across_y, "c"),
            P(),
            P(across_x, across_y),
            P(across_x, across_y, "c"),
        ),
        check_vma=False,
    )
```

```python
import functools

import jax
import jax.numpy as jnp
from jax import lax
from jax.experimental import pallas as pl
from jax.experimental.pallas import tpu as pltpu
from jax.sharding import Mesh
from jax.sharding import PartitionSpec as P

AXES = ("zl", "x", "y", "zh", "c")
SIZES = (8, 4, 4, 2, 2)
B = 8
R = 3 * B
PAD = 8
NT = 16


def linear(x, y, z, c):
    return ((((z % 8) * 4 + x) * 4 + y) * 2 + z // 8) * 2 + c


def table(place):
    out = []
    for x in range(4):
        for y in range(4):
            for z in range(16):
                for c in range(2):
                    out.append((linear(x, y, z, c), linear(*place(x, y, z, c))))
    return sorted(out)


def shifted(dx=0, dy=0, dz=0, dc=0):
    return table(lambda x, y, z, c: ((x + dx) % 4, (y + dy) % 4, (z + dz) % 16, (c + dc) % 2))


def spread(other):
    def place(x, y, z, c):
        zl, zh = z % 8, z // 8
        return (2 * zh + ((x & 1) ^ other), y, 2 * zl + (x >> 1), c)

    return table(place)


def across(x, y, z, c):
    index = (4 * y + x + (1 if c else -1)) % 16
    return (index % 4, index // 4, z, 1 - c)


def around(by):
    def place(x, y, z, c):
        index = (4 * y + x + by) % 16
        return (index % 4, index // 4, z, c)

    return table(place)


SWAP = shifted(dc=1)
ACROSS = table(across)
UP = shifted(dz=1)
DOWN = shifted(dz=-1)


def send(value, pairs):
    return lax.ppermute(value, AXES, pairs)


def back(pairs):
    return sorted((target, source) for source, target in pairs)


def merge(*parts):
    total = parts[0]
    for part in parts[1:]:
        total = jnp.where(total == 0.0, part, total)
    return total


def band():
    row = lax.broadcasted_iota(jnp.int32, (256, 256), 0)
    gap = jnp.abs(row - lax.broadcasted_iota(jnp.int32, (256, 256), 1))
    one = jnp.where(gap == 1, 16.0, jnp.where(gap == 2, -1.0, 0.0)).astype(jnp.bfloat16)
    return jnp.concatenate([one, one], axis=0)


def depth_part(buf, bands, first, count, low, size):
    field = jnp.concatenate(
        [
            buf[first : first + count, half, low : low + size, :].reshape(count * size, 128)
            for half in range(2)
        ],
        axis=1,
    )
    high = field.astype(jnp.bfloat16)
    rest = (field - high.astype(jnp.float32)).astype(jnp.bfloat16)
    return jnp.dot(
        jnp.concatenate([high, rest], axis=1), bands[...], preferred_element_type=jnp.float32
    )


def laplace_planes(buf, bands, first, count, low, size, update):
    deep = depth_part(buf, bands, first, count, low, size)
    for i in range(count):
        x = first + i
        for row in range(low, low + size, 8):
            at = i * size + row - low
            for half in range(2):
                here = buf[x, half, row : row + 8, :]
                near = (buf[x - 1, half, row : row + 8, :] + buf[x + 1, half, row : row + 8, :]) + (
                    buf[x, half, row - 1 : row + 7, :] + buf[x, half, row + 1 : row + 9, :]
                )
                far = (buf[x - 2, half, row : row + 8, :] + buf[x + 2, half, row : row + 8, :]) + (
                    buf[x, half, row - 2 : row + 6, :] + buf[x, half, row + 2 : row + 10, :]
                )
                depth = deep[at : at + 8, 128 * half : 128 * half + 128]
                update((x, half, row), (16.0 * near - far) + (depth - 90.0 * here), here)


GROUP = 4


def laplace_step(buf, bands, left, update):
    margin = 2 * left
    if left == 0:
        laplace_planes(buf, bands, B, B, PAD + 8, 8, update)
        return

    for first in range(B - margin + 2, 2 * B + margin - 2, GROUP):
        laplace_planes(buf, bands, first, GROUP, PAD, R, update)
    laplace_planes(buf, bands, B - margin, 2, PAD + 8, 8, update)
    laplace_planes(buf, bands, 2 * B + margin - 2, 2, PAD + 8, 8, update)


def assemble(buf, f, mid, intra, inter, core):
    buf[:, :, PAD + 8 : PAD + 16, :] = mid[f, :R]

    @pl.when(core == 0)
    def _():
        buf[:, :, PAD : PAD + 8, :] = inter[f, :R]
        buf[:, :, PAD + 16 : PAD + 24, :] = intra[f, :R]

    @pl.when(core == 1)
    def _():
        buf[:, :, PAD : PAD + 8, :] = intra[f, :R]
        buf[:, :, PAD + 16 : PAD + 24, :] = inter[f, :R]


def own(buf):
    return buf[B : 2 * B, :, PAD + 8 : PAD + 16, :]


def sample(buf, step, place, receivers, mine, counts, traces):
    lane = lax.broadcasted_iota(jnp.int32, (1, 128), 1)
    lanes = lax.broadcasted_iota(jnp.int32, (1, 256), 1)

    def body(i, _):
        r = mine[i]
        x = receivers[0, r] - place[0] + B
        y = receivers[1, r] - place[1] + PAD + 8
        z = receivers[2, r]
        row = buf[x, z // 128, pl.ds(y, 1), :]
        value = jnp.sum(jnp.where(lane == z % 128, row, 0.0))
        traces[step : step + 1, :] = jnp.where(lanes == r, value, traces[step : step + 1, :])
        return 0

    lax.fori_loop(0, counts[0], body, 0)


def forward_steps(steps, a, b, bands, vel, src, place, checkpoints, receivers, mine, counts, traces):
    for done, step in enumerate(steps):
        ck = checkpoints[step]

        def update(cell, lap, here, a=a, ck=ck):
            x, half, row = cell
            at = (x, half, slice(row, row + 8), slice(None))
            fixed = (x, half, slice(row - PAD, row - PAD + 8), slice(None))
            a[at] = (2.0 * here - a[at]) + (vel[fixed] * lap + src[(ck, *fixed)])

        laplace_step(b, bands, len(steps) - 1 - done, update)
        a, b = b, a
        sample(b, step, place, receivers, mine, counts, traces)
    return a, b


def first_forward(
    place, checkpoints, receivers, mine, counts, mid, intra, inter, vel, src, pair, traces, a, b, bands
):
    core = place[2]
    for f in range(5):
        into = vel if f == 0 else src.at[f - 1]
        into[:, :, 8:16, :] = mid[f]

        @pl.when(core == 0)
        def _():
            into[:, :, 0:8, :] = inter[f]
            into[:, :, 16:24, :] = intra[f]

        @pl.when(core == 1)
        def _():
            into[:, :, 0:8, :] = intra[f]
            into[:, :, 16:24, :] = inter[f]

    bands[...] = band()
    vel[...] = vel[...] * (1.0 / 12.0)
    traces[...] = jnp.zeros_like(traces)
    a[...] = jnp.zeros_like(a)
    b[:, :, PAD : PAD + R, :] = src[checkpoints[0]]
    sample(b, 0, place, receivers, mine, counts, traces)
    prev, cur = forward_steps(
        range(1, 5), a, b, bands, vel, src, place, checkpoints, receivers, mine, counts, traces
    )
    pair[0] = own(prev)
    pair[1] = own(cur)


def later_forward(
    steps, place, checkpoints, receivers, mine, counts, vel, src, mid, intra, inter, held,
    pair, traces, a, b, bands,
):
    assemble(a, 0, mid, intra, inter, place[2])
    assemble(b, 1, mid, intra, inter, place[2])
    bands[...] = band()
    traces[...] = held[...]
    prev, cur = forward_steps(
        steps, a, b, bands, vel, src, place, checkpoints, receivers, mine, counts, traces
    )
    pair[0] = own(prev)
    pair[1] = own(cur)


def inject(buf, step, place, receivers, near, counts, traces):
    lane = lax.broadcasted_iota(jnp.int32, (1, 128), 1)

    def body(i, _):
        r = near[i]
        x = (receivers[0, r] - place[0] + B) & 127
        y = ((receivers[1, r] - place[1] + B) & 255) + PAD
        z = receivers[2, r]
        half = z // 128
        row = buf[x, half, pl.ds(y, 1), :]
        buf[x, half, pl.ds(y, 1), :] = row + jnp.where(lane == z % 128, traces[step, r], 0.0)
        return 0

    lax.fori_loop(0, counts[1], body, 0)


def add_image(image, buf, back_own, ck):
    image[...] += own(buf) * back_own[ck]


def adjoint_steps(
    steps, a, b, w, bands, vel, back_own, place, checkpoints, receivers, near, counts, traces, image
):
    for done, step in enumerate(steps):
        margin = 2 * (len(steps) - 1 - done)

        for x in range(B - margin - 2, 2 * B + margin + 2):
            for row in (PAD, PAD + 8, PAD + 16):
                for half in range(2):
                    at = (x, half, slice(row, row + 8), slice(None))
                    w[at] = b[at] * vel[x, half, row - PAD : row - PAD + 8, :]

        def update(cell, lap, here, a=a, b=b):
            x, half, row = cell
            at = (x, half, slice(row, row + 8), slice(None))
            a[at] = (2.0 * b[at] - a[at]) + lap

        laplace_step(w, bands, len(steps) - 1 - done, update)
        a, b = b, a
        inject(b, step, place, receivers, near, counts, traces)
        add_image(image, b, back_own, checkpoints[step])
    return a, b


def first_adjoint(
    place, checkpoints, receivers, near, counts, traces, vel, back_own, carried, pair, image, a, b, w, bands
):
    a[...] = jnp.zeros_like(a)
    b[...] = jnp.zeros_like(b)
    image[...] = jnp.zeros_like(image)
    bands[...] = band()
    inject(b, NT - 1, place, receivers, near, counts, traces)
    add_image(image, b, back_own, checkpoints[NT - 1])
    later, now = adjoint_steps(
        range(14, 10, -1), a, b, w, bands, vel, back_own, place, checkpoints, receivers, near, counts,
        traces, image,
    )
    for f, buf in enumerate((later, now)):
        pair[f, :B] = own(buf)
        pair[f, B] = carried[f]


def later_adjoint(
    steps, place, checkpoints, receivers, near, counts, traces, vel, back_own, mid, intra, inter,
    held, far, pair, image, a, b, w, bands,
):
    assemble(a, 0, mid, intra, inter, place[2])
    assemble(b, 1, mid, intra, inter, place[2])
    image[...] = held[...]
    bands[...] = band()
    later, now = adjoint_steps(
        steps, a, b, w, bands, vel, back_own, place, checkpoints, receivers, near, counts, traces, image
    )
    for f, buf in enumerate((later, now)):
        pair[f, :B] = own(buf)
        pair[f, B] = merge(mid[f, R], intra[f, R], inter[f, R], far[f])


def list_receivers(place, receivers, mine, near, counts):
    counts[0] = 0
    counts[1] = 0

    def body(r, _):
        x = (receivers[0, r] - place[0] + B) & 127
        y = (receivers[1, r] - place[1] + B) & 255

        @pl.when((x < R) & (y < R))
        def _():
            n = counts[1]
            near[n] = r
            counts[1] = n + 1

            @pl.when((x >= B) & (x < 2 * B) & (y >= B) & (y < 2 * B))
            def _():
                m = counts[0]
                mine[m] = r
                counts[0] = m + 1

        return 0

    lax.fori_loop(0, 256, body, 0)


SM = pl.BlockSpec(memory_space=pltpu.SMEM)
VM = pl.BlockSpec(memory_space=pltpu.VMEM)
FIELD = (R, 2, R + 2 * PAD, 128)


def f32(*shape):
    return jax.ShapeDtypeStruct(shape, jnp.float32)


def i32(*shape):
    return jax.ShapeDtypeStruct(shape, jnp.int32)


def call(body, ins, outs, out_specs, fields):
    return pl.pallas_call(
        body,
        in_specs=ins,
        out_specs=out_specs,
        out_shape=outs,
        scratch_shapes=[pltpu.VMEM(FIELD, jnp.float32)] * fields
        + [pltpu.VMEM((512, 256), jnp.bfloat16)],
        compiler_params=pltpu.CompilerParams(vmem_limit_bytes=48 * 1024 * 1024),
    )


def exchange(block):
    low = send(block, UP)
    high = send(block, DOWN)
    mid = jnp.concatenate([low, block, high], axis=1)
    return mid, send(mid, SWAP), send(mid, ACROSS)


def exchange_carrying(block, jump):
    low = send(block, UP)
    high = send(block, DOWN)
    known = merge(block[:, B:], low[:, B:], high[:, B:])
    mid = jnp.concatenate([low[:, :B], block[:, :B], high[:, :B], known], axis=1)
    return (mid, send(mid, SWAP), send(mid, ACROSS)), send(mid[:, R], jump)


def pick(two, index):
    return jnp.where(index == 0, two[0], two[1])


def ordered(first, second, index, axis):
    return jnp.where(
        index == 0, jnp.stack([first, second], axis), jnp.stack([second, first], axis)
    )


def inward(stacked, core, odd):
    count = stacked.shape[0]
    rows = stacked.reshape(count, 4, 2, 2, 8, 128)
    even, uneven = rows[:, :, :, 0], rows[:, :, :, 1]
    kept = pick((even, uneven), core)
    came = send(pick((uneven, even), core), SWAP)
    whole = ordered(kept, came, core, 3)
    first, second = whole[:, :, 0], whole[:, :, 1]
    got = send(pick((first, second), odd), spread(0))
    other = send(pick((second, first), odd), spread(1))
    return ordered(got, other, odd, 1).reshape(count, 8, 2, 8, 128)


def outward_far(blocks, odd):
    first, second = blocks[:, :4], blocks[:, 4:]
    got = send(pick((first, second), odd), back(spread(0)))
    return got, send(pick((second, first), odd), back(spread(1)))


def outward_near(got, other, core, odd):
    whole = ordered(got, other, odd, 2)
    front, rear = whole[:, :, :, 0], whole[:, :, :, 1]
    kept = pick((front, rear), core)
    came = send(pick((rear, front), core), SWAP)
    return ordered(kept, came, core, 3).reshape(-1, 4, 32, 128)


def on_device(velocity_term, model_step, background, receivers, checkpoints):
    core = lax.axis_index("c")
    x = lax.axis_index("x")
    y = lax.axis_index("y")
    z = lax.axis_index("zh") * 8 + lax.axis_index("zl")
    odd = x & 1
    place = jnp.stack([B * z, 16 * (4 * y + x) + B * core, core, core]).astype(jnp.int32)
    mine, near, counts = pl.pallas_call(
        list_receivers,
        in_specs=[SM, SM],
        out_specs=[SM, SM, SM],
        out_shape=[i32(256), i32(256), i32(2)],
    )(place, receivers)
    receivers_of = (mine, near, counts)
    stacked = jnp.concatenate(
        [velocity_term[None], model_step[None], background.astype(jnp.float32)], axis=0
    )
    inner = inward(stacked, core, odd)
    back_own = inner[2:]
    fields = jnp.concatenate([inner[:1], inner[1:2] * back_own], axis=0)
    fields, (mine, near, counts) = lax.optimization_barrier((fields, receivers_of))
    vel, src, pair, traces = call(
        first_forward,
        [SM] * 5 + [VM] * 3,
        [f32(R, 2, R, 128), f32(4, R, 2, R, 128), f32(2, B, 2, B, 128), f32(NT, 256)],
        [VM] * 4,
        2,
    )(place, checkpoints, receivers, mine, counts, *exchange(fields))
    for steps in (range(5, 9), range(9, 13), range(13, 16)):
        pair, traces = call(
            functools.partial(later_forward, steps),
            [SM] * 5 + [VM] * 6,
            [f32(2, B, 2, B, 128), f32(NT, 256)],
            [VM] * 2,
            2,
        )(place, checkpoints, receivers, mine, counts, vel, src, *exchange(pair), traces)
    field = pair[1]
    local = merge(traces, send(traces, UP), send(traces, DOWN))
    local = merge(local, send(local, ACROSS), send(local, SWAP))
    carried = local.reshape(2, 8, 2, 128).transpose(0, 2, 1, 3)
    scalars = (place, checkpoints, receivers, near, counts, local)
    outs = [f32(2, B + 1, 2, B, 128), f32(B, 2, B, 128)]
    pair, image = call(first_adjoint, [SM] * 6 + [VM] * 3, outs, [VM] * 2, 3)(
        *scalars, vel, back_own, carried
    )
    jumps = (around(3), around(-3), shifted(dz=8))
    for steps, jump in zip((range(10, 6, -1), range(6, 2, -1), range(2, -1, -1)), jumps):
        parts, more = exchange_carrying(pair, jump)
        pair, image = call(
            functools.partial(later_adjoint, steps), [SM] * 6 + [VM] * 7, outs, [VM] * 2, 3
        )(*scalars, vel, back_own, *parts, image, more if steps.stop > -1 else carried)
    image, wavefield = outward_near(*outward_far(jnp.stack([image, field]), odd), core, odd)
    carried = merge(pair[:, B], more)
    carried = merge(carried, send(carried, shifted(dy=2)))
    traces = carried.transpose(0, 2, 1, 3).reshape(NT, 256)
    column_image = lax.psum(jnp.sum(image, axis=2), "c") / 256.0
    return (image, traces, column_image, wavefield)


def solution(mesh):
    torus = Mesh(mesh.devices.reshape(SIZES), AXES)
    across_x, across_y = ("zl", "x"), ("y", "zh")
    return jax.shard_map(
        on_device,
        mesh=torus,
        in_specs=(
            P(across_x, across_y, "c"),
            P(across_x, across_y, "c"),
            P(None, across_x, across_y, "c"),
            P(),
            P(),
        ),
        out_specs=(
            P(across_x, across_y, "c"),
            P(),
            P(across_x, across_y),
            P(across_x, across_y, "c"),
        ),
        check_vma=False,
    )
```

```python
import functools

import jax
import jax.numpy as jnp
from jax import lax
from jax.experimental import pallas as pl
from jax.experimental.pallas import tpu as pltpu
from jax.sharding import Mesh
from jax.sharding import PartitionSpec as P

AXES = ("zl", "x", "y", "zh", "c")
SIZES = (8, 4, 4, 2, 2)
B = 8
R = 3 * B
PAD = 8
NT = 16


def linear(x, y, z, c):
    return ((((z % 8) * 4 + x) * 4 + y) * 2 + z // 8) * 2 + c


def table(place):
    out = []
    for x in range(4):
        for y in range(4):
            for z in range(16):
                for c in range(2):
                    out.append((linear(x, y, z, c), linear(*place(x, y, z, c))))
    return sorted(out)


def shifted(dx=0, dy=0, dz=0, dc=0):
    return table(lambda x, y, z, c: ((x + dx) % 4, (y + dy) % 4, (z + dz) % 16, (c + dc) % 2))


def spread(other):
    def place(x, y, z, c):
        zl, zh = z % 8, z // 8
        return (2 * zh + ((x & 1) ^ other), y, 2 * zl + (x >> 1), c)

    return table(place)


def beside(x, y, z, c):
    index = (4 * y + x + (1 if c else -1)) % 16
    return (index % 4, index // 4, z, 1 - c)


def around(by):
    def place(x, y, z, c):
        index = (4 * y + x + by) % 16
        return (index % 4, index // 4, z, c)

    return table(place)


SWAP = shifted(dc=1)
ACROSS = table(beside)
UP = shifted(dz=1)
DOWN = shifted(dz=-1)


def send(value, pairs):
    return lax.ppermute(value, AXES, pairs)


def back(pairs):
    return sorted((target, source) for source, target in pairs)


def merge(*parts):
    total = parts[0]
    for part in parts[1:]:
        total = jnp.where(total == 0.0, part, total)
    return total


def band():
    row = lax.broadcasted_iota(jnp.int32, (256, 256), 0)
    gap = jnp.abs(row - lax.broadcasted_iota(jnp.int32, (256, 256), 1))
    one = jnp.where(gap == 1, 16.0, jnp.where(gap == 2, -1.0, 0.0)).astype(jnp.bfloat16)
    return jnp.concatenate([one, one], axis=0)


def depth_part(buf, bands, first, count, low, size):
    field = jnp.concatenate(
        [
            buf[first : first + count, half, low : low + size, :].reshape(count * size, 128)
            for half in range(2)
        ],
        axis=1,
    )
    high = field.astype(jnp.bfloat16)
    rest = (field - high.astype(jnp.float32)).astype(jnp.bfloat16)
    return jnp.dot(
        jnp.concatenate([high, rest], axis=1), bands[...], preferred_element_type=jnp.float32
    )


def laplace_planes(buf, bands, first, count, low, size, update):
    deep = depth_part(buf, bands, first, count, low, size)
    for i in range(count):
        x = first + i
        for row in range(low, low + size, 8):
            at = i * size + row - low
            for half in range(2):
                here = buf[x, half, row : row + 8, :]
                near = (buf[x - 1, half, row : row + 8, :] + buf[x + 1, half, row : row + 8, :]) + (
                    buf[x, half, row - 1 : row + 7, :] + buf[x, half, row + 1 : row + 9, :]
                )
                far = (buf[x - 2, half, row : row + 8, :] + buf[x + 2, half, row : row + 8, :]) + (
                    buf[x, half, row - 2 : row + 6, :] + buf[x, half, row + 2 : row + 10, :]
                )
                depth = deep[at : at + 8, 128 * half : 128 * half + 128]
                update((x, half, row), (16.0 * near - far) + (depth - 90.0 * here), here)


GROUP = 4


def laplace_step(buf, bands, left, update):
    margin = 2 * left
    if left == 0:
        laplace_planes(buf, bands, B, B, PAD + 8, 8, update)
        return

    for first in range(B - margin + 2, 2 * B + margin - 2, GROUP):
        laplace_planes(buf, bands, first, GROUP, PAD, R, update)
    laplace_planes(buf, bands, B - margin, 2, PAD + 8, 8, update)
    laplace_planes(buf, bands, 2 * B + margin - 2, 2, PAD + 8, 8, update)


PAIRS = ((1, 5, 6), (2, 6, 6), (3, 4, 4))
PACKED = B + 2 * len(PAIRS)


def side_planes():
    for side in range(2):
        for i, (one, two, rows) in enumerate(PAIRS):
            tile = B + len(PAIRS) * side + i
            planes = [B - d if side == 0 else 2 * B - 1 + d for d in (one, two)]
            yield tile, planes[0], planes[1], rows


def pack_first_rows(to, f, mid):
    for tile, one, two, rows in side_planes():
        to[f, tile, :, :rows] = mid[f, one, :, :rows]
        to[f, tile, :, rows:] = mid[f, two, :, : 8 - rows]


def pack_last_rows(to, f, mid):
    for tile, one, two, rows in side_planes():
        to[f, tile, :, 8 - rows :] = mid[f, one, :, 8 - rows :]
        to[f, tile, :, : 8 - rows] = mid[f, two, :, rows:]


def pack(count, place, low, block, high, mid, swapped, across):
    for f in range(count):
        mid[f, :B] = low[f, :B]
        mid[f, B : 2 * B] = block[f, :B]
        mid[f, 2 * B : R] = high[f, :B]
        swapped[f, :B] = block[f, :B]
        across[f, :B] = block[f, :B]
        if block.shape[1] > B:
            known = merge(block[f, B], low[f, B], high[f, B])
            mid[f, R] = known
            swapped[f, PACKED] = known
            across[f, PACKED] = known

    @pl.when(place[2] == 0)
    def _():
        for f in range(count):
            pack_first_rows(across, f, mid)
            pack_last_rows(swapped, f, mid)

    @pl.when(place[2] == 1)
    def _():
        for f in range(count):
            pack_last_rows(across, f, mid)
            pack_first_rows(swapped, f, mid)


def unpack_below(buf, base, f, came):
    buf[B : 2 * B, :, base : base + 8, :] = came[f, :B]
    for tile, one, two, rows in side_planes():
        buf[one, :, base + 8 - rows : base + 8, :] = came[f, tile, :, 8 - rows :]
        buf[two, :, base + rows : base + 8, :] = came[f, tile, :, : 8 - rows]


def unpack_above(buf, base, f, came):
    buf[B : 2 * B, :, base + 16 : base + 24, :] = came[f, :B]
    for tile, one, two, rows in side_planes():
        buf[one, :, base + 16 : base + 16 + rows, :] = came[f, tile, :, :rows]
        buf[two, :, base + 16 : base + 24 - rows, :] = came[f, tile, :, rows:]


def assemble(buf, base, f, mid, inter, intra, core):
    buf[:, :, base + 8 : base + 16, :] = mid[f, :R]

    @pl.when(core == 0)
    def _():
        unpack_below(buf, base, f, inter)
        unpack_above(buf, base, f, intra)

    @pl.when(core == 1)
    def _():
        unpack_below(buf, base, f, intra)
        unpack_above(buf, base, f, inter)


def own(buf):
    return buf[B : 2 * B, :, PAD + 8 : PAD + 16, :]


def sample(buf, step, place, receivers, mine, counts, traces):
    lane = lax.broadcasted_iota(jnp.int32, (1, 128), 1)
    lanes = lax.broadcasted_iota(jnp.int32, (1, 256), 1)

    def body(i, _):
        r = mine[i]
        x = receivers[0, r] - place[0] + B
        y = receivers[1, r] - place[1] + PAD + 8
        z = receivers[2, r]
        row = buf[x, z // 128, pl.ds(y, 1), :]
        value = jnp.sum(jnp.where(lane == z % 128, row, 0.0))
        traces[step : step + 1, :] = jnp.where(lanes == r, value, traces[step : step + 1, :])
        return 0

    lax.fori_loop(0, counts[0], body, 0)


def forward_steps(steps, a, b, bands, vel, src, place, checkpoints, receivers, mine, counts, traces):
    for done, step in enumerate(steps):
        ck = checkpoints[step]

        def update(cell, lap, here, a=a, ck=ck):
            x, half, row = cell
            at = (x, half, slice(row, row + 8), slice(None))
            fixed = (x, half, slice(row - PAD, row - PAD + 8), slice(None))
            a[at] = (2.0 * here - a[at]) + (vel[fixed] * lap + src[(ck, *fixed)])

        laplace_step(b, bands, len(steps) - 1 - done, update)
        a, b = b, a
        sample(b, step, place, receivers, mine, counts, traces)
    return a, b


def first_forward(
    place, checkpoints, receivers, mine, counts, mid, inter, intra, vel, src, pair, traces, a, b, bands
):
    vel[...] = jnp.zeros_like(vel)
    src[...] = jnp.zeros_like(src)
    for f in range(5):
        assemble(vel if f == 0 else src.at[f - 1], 0, f, mid, inter, intra, place[2])
    bands[...] = band()
    vel[...] = vel[...] * (1.0 / 12.0)
    traces[...] = jnp.zeros_like(traces)
    a[...] = jnp.zeros_like(a)
    b[:, :, PAD : PAD + R, :] = src[checkpoints[0]]
    sample(b, 0, place, receivers, mine, counts, traces)
    prev, cur = forward_steps(
        range(1, 5), a, b, bands, vel, src, place, checkpoints, receivers, mine, counts, traces
    )
    pair[0] = own(prev)
    pair[1] = own(cur)


def later_forward(
    steps, place, checkpoints, receivers, mine, counts, vel, src, mid, inter, intra, held,
    pair, traces, a, b, bands,
):
    assemble(a, PAD, 0, mid, inter, intra, place[2])
    assemble(b, PAD, 1, mid, inter, intra, place[2])
    bands[...] = band()
    traces[...] = held[...]
    prev, cur = forward_steps(
        steps, a, b, bands, vel, src, place, checkpoints, receivers, mine, counts, traces
    )
    pair[0] = own(prev)
    pair[1] = own(cur)


def inject(buf, step, place, receivers, near, counts, traces):
    lane = lax.broadcasted_iota(jnp.int32, (1, 128), 1)

    def body(i, _):
        r = near[i]
        x = (receivers[0, r] - place[0] + B) & 127
        y = ((receivers[1, r] - place[1] + B) & 255) + PAD
        z = receivers[2, r]
        half = z // 128
        row = buf[x, half, pl.ds(y, 1), :]
        buf[x, half, pl.ds(y, 1), :] = row + jnp.where(lane == z % 128, traces[step, r], 0.0)
        return 0

    lax.fori_loop(0, counts[1], body, 0)


def add_image(image, buf, back_own, ck):
    image[...] += own(buf) * back_own[ck]


def adjoint_steps(
    steps, a, b, w, bands, vel, back_own, place, checkpoints, receivers, near, counts, traces, image
):
    for done, step in enumerate(steps):
        margin = 2 * (len(steps) - 1 - done)

        for x in range(B - margin - 2, 2 * B + margin + 2):
            for row in (PAD, PAD + 8, PAD + 16):
                for half in range(2):
                    at = (x, half, slice(row, row + 8), slice(None))
                    w[at] = b[at] * vel[x, half, row - PAD : row - PAD + 8, :]

        def update(cell, lap, here, a=a, b=b):
            x, half, row = cell
            at = (x, half, slice(row, row + 8), slice(None))
            a[at] = (2.0 * b[at] - a[at]) + lap

        laplace_step(w, bands, len(steps) - 1 - done, update)
        a, b = b, a
        inject(b, step, place, receivers, near, counts, traces)
        add_image(image, b, back_own, checkpoints[step])
    return a, b


def first_adjoint(
    place, checkpoints, receivers, near, counts, traces, vel, back_own, carried, pair, image, a, b, w, bands
):
    a[...] = jnp.zeros_like(a)
    b[...] = jnp.zeros_like(b)
    image[...] = jnp.zeros_like(image)
    bands[...] = band()
    inject(b, NT - 1, place, receivers, near, counts, traces)
    add_image(image, b, back_own, checkpoints[NT - 1])
    later, now = adjoint_steps(
        range(14, 10, -1), a, b, w, bands, vel, back_own, place, checkpoints, receivers, near, counts,
        traces, image,
    )
    for f, buf in enumerate((later, now)):
        pair[f, :B] = own(buf)
        pair[f, B] = carried[f]


def later_adjoint(
    steps, place, checkpoints, receivers, near, counts, traces, vel, back_own, mid, inter, intra,
    held, far, pair, image, a, b, w, bands,
):
    assemble(a, PAD, 0, mid, inter, intra, place[2])
    assemble(b, PAD, 1, mid, inter, intra, place[2])
    image[...] = held[...]
    bands[...] = band()
    later, now = adjoint_steps(
        steps, a, b, w, bands, vel, back_own, place, checkpoints, receivers, near, counts, traces, image
    )
    for f, buf in enumerate((later, now)):
        pair[f, :B] = own(buf)
        pair[f, B] = merge(mid[f, R], intra[f, PACKED], inter[f, PACKED], far[f])


def list_receivers(place, receivers, mine, near, counts):
    counts[0] = 0
    counts[1] = 0

    def body(r, _):
        x = (receivers[0, r] - place[0] + B) & 127
        y = (receivers[1, r] - place[1] + B) & 255

        @pl.when((x < R) & (y < R))
        def _():
            n = counts[1]
            near[n] = r
            counts[1] = n + 1

            @pl.when((x >= B) & (x < 2 * B) & (y >= B) & (y < 2 * B))
            def _():
                m = counts[0]
                mine[m] = r
                counts[0] = m + 1

        return 0

    lax.fori_loop(0, 256, body, 0)


SM = pl.BlockSpec(memory_space=pltpu.SMEM)
VM = pl.BlockSpec(memory_space=pltpu.VMEM)
FIELD = (R, 2, R + 2 * PAD, 128)


def f32(*shape):
    return jax.ShapeDtypeStruct(shape, jnp.float32)


def i32(*shape):
    return jax.ShapeDtypeStruct(shape, jnp.int32)


def call(body, ins, outs, out_specs, fields):
    return pl.pallas_call(
        body,
        in_specs=ins,
        out_specs=out_specs,
        out_shape=outs,
        scratch_shapes=[pltpu.VMEM(FIELD, jnp.float32)] * fields
        + [pltpu.VMEM((512, 256), jnp.bfloat16)],
        compiler_params=pltpu.CompilerParams(vmem_limit_bytes=48 * 1024 * 1024),
    )


def exchange(block, place, jump=None):
    count, planes = block.shape[:2]
    small = f32(count, planes + PACKED - B, 2, B, 128)
    mid, swapped, across = pl.pallas_call(
        functools.partial(pack, count),
        in_specs=[SM] + [VM] * 3,
        out_specs=[VM] * 3,
        out_shape=[f32(count, planes + R - B, 2, B, 128), small, small],
        compiler_params=pltpu.CompilerParams(vmem_limit_bytes=48 * 1024 * 1024),
    )(place, send(block, UP), block, send(block, DOWN))
    parts = (mid, send(across, ACROSS), send(swapped, SWAP))
    return parts if jump is None else (parts, send(mid[:, R], jump))


def pick(two, index):
    return jnp.where(index == 0, two[0], two[1])


def ordered(first, second, index, axis):
    return jnp.where(
        index == 0, jnp.stack([first, second], axis), jnp.stack([second, first], axis)
    )


def inward(stacked, core, odd):
    count = stacked.shape[0]
    rows = stacked.reshape(count, 4, 2, 2, 8, 128)
    even, uneven = rows[:, :, :, 0], rows[:, :, :, 1]
    kept = pick((even, uneven), core)
    came = send(pick((uneven, even), core), SWAP)
    whole = ordered(kept, came, core, 3)
    first, second = whole[:, :, 0], whole[:, :, 1]
    got = send(pick((first, second), odd), spread(0))
    other = send(pick((second, first), odd), spread(1))
    return ordered(got, other, odd, 1).reshape(count, 8, 2, 8, 128)


def outward_far(blocks, odd):
    first, second = blocks[:, :4], blocks[:, 4:]
    got = send(pick((first, second), odd), back(spread(0)))
    return got, send(pick((second, first), odd), back(spread(1)))


def outward_near(got, other, core, odd):
    whole = ordered(got, other, odd, 2)
    column = jnp.sum(whole[0], axis=(2, 4)) / 256.0
    spread_out = jnp.broadcast_to(column[None, ..., None], (1, *column.shape, 128))
    front, rear = whole[:, :, :, 0], whole[:, :, :, 1]
    kept = pick((front, rear), core)
    came = send(jnp.concatenate([pick((rear, front), core), spread_out], axis=0), SWAP)
    column = ordered(column, came[-1, ..., 0], core, 2).reshape(4, 32)
    return *ordered(kept, came[:-1], core, 3).reshape(-1, 4, 32, 128), column


def on_device(velocity_term, model_step, background, receivers, checkpoints):
    core = lax.axis_index("c")
    x = lax.axis_index("x")
    y = lax.axis_index("y")
    z = lax.axis_index("zh") * 8 + lax.axis_index("zl")
    odd = x & 1
    place = jnp.stack([B * z, 16 * (4 * y + x) + B * core, core, core]).astype(jnp.int32)
    mine, near, counts = pl.pallas_call(
        list_receivers,
        in_specs=[SM, SM],
        out_specs=[SM, SM, SM],
        out_shape=[i32(256), i32(256), i32(2)],
    )(place, receivers)
    receivers_of = (mine, near, counts)
    stacked = jnp.concatenate(
        [velocity_term[None], model_step[None], background.astype(jnp.float32)], axis=0
    )
    inner = inward(stacked, core, odd)
    back_own = inner[2:]
    fields = jnp.concatenate([inner[:1], inner[1:2] * back_own], axis=0)
    fields, (mine, near, counts) = lax.optimization_barrier((fields, receivers_of))
    vel, src, pair, traces = call(
        first_forward,
        [SM] * 5 + [VM] * 3,
        [f32(R, 2, R, 128), f32(4, R, 2, R, 128), f32(2, B, 2, B, 128), f32(NT, 256)],
        [VM] * 4,
        2,
    )(place, checkpoints, receivers, mine, counts, *exchange(fields, place))
    for steps in (range(5, 9), range(9, 13), range(13, 16)):
        pair, traces = call(
            functools.partial(later_forward, steps),
            [SM] * 5 + [VM] * 6,
            [f32(2, B, 2, B, 128), f32(NT, 256)],
            [VM] * 2,
            2,
        )(place, checkpoints, receivers, mine, counts, vel, src, *exchange(pair, place), traces)
    field = pair[1]
    local = merge(traces, send(traces, UP), send(traces, DOWN))
    local = merge(local, send(local, ACROSS), send(local, SWAP))
    carried = local.reshape(2, 8, 2, 128).transpose(0, 2, 1, 3)
    scalars = (place, checkpoints, receivers, near, counts, local)
    outs = [f32(2, B + 1, 2, B, 128), f32(B, 2, B, 128)]
    pair, image = call(first_adjoint, [SM] * 6 + [VM] * 3, outs, [VM] * 2, 3)(
        *scalars, vel, back_own, carried
    )
    jumps = (around(3), around(-3), shifted(dz=8))
    for steps, jump in zip((range(10, 6, -1), range(6, 2, -1), range(2, -1, -1)), jumps):
        parts, more = exchange(pair, place, jump)
        pair, image = call(
            functools.partial(later_adjoint, steps), [SM] * 6 + [VM] * 7, outs, [VM] * 2, 3
        )(*scalars, vel, back_own, *parts, image, more if steps.stop > -1 else carried)
    got, other = outward_far(jnp.stack([image, field]), odd)
    got, last, more = lax.optimization_barrier((got, pair[:, B], more))
    image, wavefield, column_image = outward_near(got, other, core, odd)
    carried = merge(last, more)
    carried = merge(carried, send(carried, shifted(dy=2)))
    traces = carried.transpose(0, 2, 1, 3).reshape(NT, 256)
    return (image, traces, column_image, wavefield)


def solution(mesh):
    torus = Mesh(mesh.devices.reshape(SIZES), AXES)
    across_x, across_y = ("zl", "x"), ("y", "zh")
    return jax.shard_map(
        on_device,
        mesh=torus,
        in_specs=(
            P(across_x, across_y, "c"),
            P(across_x, across_y, "c"),
            P(None, across_x, across_y, "c"),
            P(),
            P(),
        ),
        out_specs=(
            P(across_x, across_y, "c"),
            P(),
            P(across_x, across_y),
            P(across_x, across_y, "c"),
        ),
        check_vma=False,
    )
```
